32 devices in a mesh: dp: 8 (over z, x), ctx: 4 (over y, core).
Axes of the slice: x: 2, y: 2, z: 4, core: 2. Of those that a mesh axis runs over, the one named last changes fastest.
Arguments:
- hidden: bfloat16 [2, 8192, 1024], P(None, ('dp', 'ctx')), may hold values from -6 to 6
- cotangent: bfloat16 [2, 8192, 1024], P(None, ('dp', 'ctx')), may hold values from -6 to 6
- seq_lengths: int32 [8, 2, 1], P('dp'), may hold values from 512 to 1024, as said below
- norm_gain: bfloat16 [1024], P(('dp', 'ctx')), may hold values from 0.099609375 to 1.8984375
- in_proj: bfloat16 [1024, 3352], P(('dp', 'ctx')), may hold values from -1 to 1
- conv_weight: bfloat16 [4, 1792], P(None, ('dp', 'ctx')), may hold values from -3 to 3
- conv_bias: bfloat16 [1792], P(('dp', 'ctx')), may hold values from -3 to 3
- gate_gain: bfloat16 [1536], P(('dp', 'ctx')), may hold values from 0.099609375 to 1.8984375
- out_proj: bfloat16 [1536, 1024], P(('dp', 'ctx')), may hold values from -0.15625 to 0.15625
- q_proj: bfloat16 [1024, 512], P(('dp', 'ctx')), may hold values from -0.1875 to 0.1875
- kv_proj: bfloat16 [1024, 256], P(('dp', 'ctx')), may hold values from -0.1875 to 0.1875
- o_proj: bfloat16 [512, 1024], P(('dp', 'ctx')), may hold values from -2 to 2
- ff_gain: bfloat16 [1024], P(('dp', 'ctx')), may hold values from 0.099609375 to 1.8984375
- gate_up: bfloat16 [1024, 4096], P(('dp', 'ctx')), may hold values from -0.1875 to 0.1875
- down_proj: bfloat16 [2048, 1024], P(('dp', 'ctx')), may hold values from -0.125 to 0.125
- a_log: float32 [24], replicated, may hold values from -3.5 to 0.5
- dt_bias: float32 [24], replicated, may hold values from -4.5 to -2.5
- skip_scale: float32 [24], replicated, may hold values from 0.25 to 1
Outputs:
- layer_out: bfloat16 [2, 8192, 1024], P(None, ('dp', 'ctx'))
- grad_hidden: bfloat16 [2, 8192, 1024], P(None, ('dp', 'ctx'))
- grad_norm_gain: float32 [1024], P(('dp', 'ctx'))
- grad_in_proj: float32 [1024, 3352], P(('dp', 'ctx'))
- grad_conv_weight: float32 [4, 1792], P(None, ('dp', 'ctx'))
- grad_conv_bias: float32 [1792], P(('dp', 'ctx'))
- grad_gate_gain: float32 [1536], P(('dp', 'ctx'))
- grad_out_proj: float32 [1536, 1024], P(('dp', 'ctx'))
- grad_q_proj: float32 [1024, 512], P(('dp', 'ctx'))
- grad_kv_proj: float32 [1024, 256], P(('dp', 'ctx'))
- grad_o_proj: float32 [512, 1024], P(('dp', 'ctx'))
- grad_ff_gain: float32 [1024], P(('dp', 'ctx'))
- grad_gate_up: float32 [1024, 4096], P(('dp', 'ctx'))
- grad_down_proj: float32 [2048, 1024], P(('dp', 'ctx'))
- grad_a_log: float32 [24], replicated
- grad_dt_bias: float32 [24], replicated
- grad_skip_scale: float32 [24], replicated
The draws below stay inside these ranges and needn't reach their ends.
Inputs may be any that keep to these rules, and one draw needn't show every extreme that they name: `seq_lengths`: in each group and micro-batch the given sequences come first, then zeros; there is at least one sequence; a nonzero length lies between 512 and 1024 and is a multiple of the number of devices along ctx; the lengths of one group and micro-batch sum to at most 1024, and some group and micro-batch reach that sum.
All inputs are finite; a program needn't handle non-finite values.
Results may differ from the reference program's by a relative error of at most 0.038.
Values may be sent and summed in bfloat16 or wider, within the bound.
A program may use at most 256 MiB of HBM per device.

```python
import jax
import jax.numpy as jnp
from jax import lax

D = 1024
MH = 24
HP = 64
NS = 128
CONV = 4
AH = 8
KVH = 2
AD = 64
FF = 2048
MICRO = 2
TOK_DEV = 256
SEQ_MAX = 1024
DI = 1536
XC = 1792
ZW = 3352
QD = 512
KD = 128
QMIN = 128
QMAX = 256
SEQS = 1
GROUPS = 8
TOKENS = 8192
N_DP = 8
N_CTX = 4


def draw_seq_lengths(key, part):
    key = jax.random.fold_in(key, 17)
    subkeys = jax.random.split(key, 4)
    pair_count = GROUPS * MICRO
    fewest = max(1, SEQS // 2)
    span_len = jax.random.randint(subkeys[0], (pair_count, SEQS), QMIN, QMAX + 1)
    live_count = jax.random.randint(subkeys[1], (pair_count,), fewest, SEQS + 1)
    full_pair = jax.random.randint(subkeys[2], (), 0, pair_count)
    short_pair = (full_pair + jax.random.randint(subkeys[3], (), 1, pair_count)) % pair_count
    pair_index = jnp.arange(pair_count)
    live_count = jnp.where(pair_index == full_pair, SEQS, jnp.where(pair_index == short_pair, fewest, live_count))
    slot_index = jnp.arange(SEQS)[None, :]
    span_len = jnp.where(pair_index[:, None] == full_pair, QMAX, span_len)
    span_len = jnp.where((pair_index[:, None] == short_pair) & (slot_index == 0), QMIN, span_len)
    lengths = jnp.where(slot_index < live_count[:, None], span_len * (SEQ_MAX // QMAX), 0)
    return lengths.reshape(MICRO, GROUPS, SEQS).transpose(1, 0, 2).astype(jnp.int32)


def draw_in_proj(key, part):
    key = jax.random.fold_in(key, 23)
    base = jax.random.normal(key, (D, ZW), jnp.float32) * D ** (-0.5)
    column = jnp.arange(ZW)[None, :]
    widened = jnp.where(column >= ZW - MH, 4.0 * base, base)
    return jnp.clip(widened, -1.0, 1.0).astype(jnp.bfloat16)


def steps_of(stream_key, shape, cuts, smallest, high):
    def one(axis_at, shards_of):
        heights = jax.random.uniform(jax.random.fold_in(jax.random.fold_in(stream_key, 6), axis_at), (shards_of,), jnp.float32, smallest / len(cuts), high / len(cuts))
        return jnp.repeat(jnp.exp(heights), shape[axis_at] // shards_of).reshape((-1,) + (1,) * (len(shape) - axis_at - 1))

    factor_of = one(*cuts[0])
    for cut in cuts[1:]:
        factor_of = factor_of * one(*cut)
    return factor_of


def normal_values(stream_key, shape, deviation, most, cuts=(), kind=jnp.bfloat16):
    drawn = deviation * jax.random.normal(stream_key, shape, jnp.float32)
    if cuts:
        drawn = drawn * steps_of(stream_key, shape, cuts, -0.22, 0.18)
    return jnp.clip(drawn, -most, most).astype(kind)


def setup_inputs(seed: int = 0) -> dict:
    seeds = jax.random.split(jax.random.key(seed), 19)
    return {
        "hidden": normal_values(seeds[0], (MICRO, TOKENS, D), 1.0, 6.0, ((1, 32),)),
        "cotangent": normal_values(seeds[1], (MICRO, TOKENS, D), 1.0, 6.0, ((1, 32),)),
        "seq_lengths": draw_seq_lengths(jax.random.fold_in(seeds[18], 71), 0),
        "norm_gain": jnp.clip(1.0 + 0.18 * jax.random.normal(seeds[3], (D,), jnp.float32), 0.099609375, 1.8984375).astype(jnp.bfloat16),
        "in_proj": draw_in_proj(jax.random.fold_in(seeds[18], 71), 0),
        "conv_weight": normal_values(seeds[5], (CONV, XC), CONV ** -0.5, 3.0, ((1, 32),)),
        "conv_bias": normal_values(seeds[6], (XC,), 0.5, 3.0, ((0, 32),)),
        "gate_gain": jnp.clip(1.0 + 0.18 * jax.random.normal(seeds[7], (DI,), jnp.float32), 0.099609375, 1.8984375).astype(jnp.bfloat16),
        "out_proj": normal_values(seeds[8], (DI, D), DI ** -0.5, 0.15625, ((0, 32),)),
        "q_proj": normal_values(seeds[9], (D, QD), D ** -0.5, 0.1875, ((0, 32),)),
        "kv_proj": normal_values(seeds[10], (D, 2 * KD), D ** -0.5, 0.1875, ((0, 32),)),
        "o_proj": normal_values(seeds[11], (QD, D), 8 ** -0.5, 2.0, ((0, 32),)),
        "ff_gain": jnp.clip(1.0 + 0.18 * jax.random.normal(seeds[12], (D,), jnp.float32), 0.099609375, 1.8984375).astype(jnp.bfloat16),
        "gate_up": normal_values(seeds[13], (D, 2 * FF), D ** -0.5, 0.1875, ((0, 32),)),
        "down_proj": normal_values(seeds[14], (FF, D), FF ** -0.5, 0.125, ((0, 32),)),
        "a_log": jnp.clip(jax.random.uniform(seeds[15], (MH,), jnp.float32, -3.5, 0.5), -3.5, 0.5),
        "dt_bias": jnp.clip(jax.random.uniform(seeds[16], (MH,), jnp.float32, -4.5, -2.5), -4.5, -2.5),
        "skip_scale": jnp.clip(jax.random.uniform(seeds[17], (MH,), jnp.float32, 0.25, 1.0), 0.25, 1.0),
    }


EPSILON = 1e-05
HIGHEST = lax.Precision.HIGHEST
MASKED = -1e+30

@jax.custom_vjp
def low(v):
    return lax.optimization_barrier(v.astype(jnp.bfloat16)).astype(jnp.float32)

@jax.custom_vjp
def low_back(v):
    return v

def low_keep(v):
    return (low(v), None)

def low_pass(kept, grad):
    return (grad,)

def back_keep(v):
    return (v, None)

def back_low(kept, grad):
    return (low(grad),)
low.defvjp(low_keep, low_pass)
low_back.defvjp(back_keep, back_low)

def product(first_arg, second_arg):
    return jnp.dot(first_arg, second_arg, precision=HIGHEST, preferred_element_type=jnp.float32)

def rms_scale(signal, scale):
    return signal * lax.rsqrt(lax.optimization_barrier(jnp.mean(signal * signal, axis=-1, keepdims=True)) + EPSILON) * scale

def row_layout(span_len, row_count):
    seq_ends = jnp.cumsum(span_len).astype(jnp.int32)
    filled = seq_ends[-1]
    local_row = jnp.arange(row_count, dtype=jnp.int32)
    passed = local_row[:, None] >= seq_ends[None, :]
    segment = lax.optimization_barrier(jnp.sum(passed.astype(jnp.int32), axis=1)).astype(jnp.int32)
    start_row = lax.optimization_barrier(jnp.sum(jnp.where(passed, span_len[None, :], 0), axis=1)).astype(jnp.int32)
    slot_count = span_len.shape[0]
    owner = segment[:, None] == jnp.arange(slot_count, dtype=jnp.int32)[None, :]
    extent = (lax.optimization_barrier(jnp.sum(jnp.where(owner, span_len[None, :], 0), axis=1)) + jnp.where(segment == slot_count, row_count - filled, 0)).astype(jnp.int32)
    offset = (local_row - start_row).astype(jnp.int32)
    alive_row = (local_row < filled).astype(jnp.float32)
    return (segment, offset, extent, start_row, alive_row)

def causal_conv(signal, conv_weight, conv_bias, position):
    length = signal.shape[0]
    result = conv_bias[None, :] + conv_weight[CONV - 1][None, :] * signal
    for shift_by in range(1, CONV):
        shifted = jnp.concatenate([jnp.zeros((shift_by, signal.shape[1]), jnp.float32), signal[:length - shift_by]], axis=0)
        result = result + jnp.where((position >= shift_by)[:, None], shifted, 0.0) * conv_weight[CONV - 1 - shift_by][None, :]
    return result

def state_space(values, step_size, log_decay, b_in, c_out, segment, skip_scale):
    length = values.shape[0]
    block_rows = min(256, length)
    scaled = values * step_size[:, :, None]

    def blocks(array):
        return array.reshape((length // block_rows, block_rows) + array.shape[1:])

    def advance(carry, pieces):
        carry_state, before = carry
        piece_x, piece_decay, piece_b, piece_c, piece_seg = pieces
        cumul = jnp.cumsum(piece_decay, axis=0)
        row_order = jnp.arange(block_rows, dtype=jnp.int32)
        allowed = (row_order[:, None] >= row_order[None, :]) & (piece_seg[:, None] == piece_seg[None, :])
        decay_mat = jnp.where(allowed[:, :, None], jnp.exp(jnp.minimum(cumul[:, None, :] - cumul[None, :, :], 0.0)), 0.0)
        inner_cb = product(piece_c, piece_b.T)
        within = jnp.einsum('tsh,shp->thp', decay_mat * inner_cb[:, :, None], piece_x, precision=HIGHEST)
        carried = jnp.einsum('tn,hpn->thp', piece_c, carry_state, precision=HIGHEST)
        carried = carried * (jnp.exp(cumul) * (piece_seg == before).astype(jnp.float32)[:, None])[:, :, None]
        last_seg = piece_seg[block_rows - 1]
        toward = jnp.exp(cumul[block_rows - 1][None, :] - cumul) * (piece_seg == last_seg).astype(jnp.float32)[:, None]
        fresh_state = jnp.einsum('th,thp,tn->hpn', toward, piece_x, piece_b, precision=HIGHEST)
        kept_state = carry_state * (jnp.exp(cumul[block_rows - 1]) * (last_seg == before).astype(jnp.float32))[:, None, None]
        return ((fresh_state + kept_state, last_seg), within + carried)
    initial = (jnp.zeros((MH, HP, NS), jnp.float32), jnp.int32(-1))
    _, outputs = lax.scan(jax.checkpoint(advance), initial, (blocks(scaled), blocks(log_decay), blocks(b_in), blocks(c_out), blocks(segment)))
    return outputs.reshape(length, MH, HP) + skip_scale[None, :, None] * values

def attention(queries, keyvals, segment, position):
    length = queries.shape[0]
    block_rows = min(512, length)
    groups = AH // KVH
    key_heads = keyvals[:, :KD].reshape(length, KVH, AD)
    value_heads = keyvals[:, KD:].reshape(length, KVH, AD)

    def attend_block(pieces):
        query_piece, seg_piece, pos_piece = pieces
        raw_score = jnp.einsum('tgjd,sgd->tgjs', query_piece, key_heads, precision=HIGHEST) * AD ** (-0.5)
        scores = low_back(raw_score)
        allowed = (seg_piece[:, None] == segment[None, :]) & (pos_piece[:, None] >= position[None, :])
        scores = jnp.where(allowed[:, None, None, :], scores, MASKED)
        weights = low(jax.nn.softmax(scores, axis=-1))
        return jnp.einsum('tgjs,sgd->tgjd', weights, value_heads, precision=HIGHEST).reshape(block_rows, QD)
    nblocks = length // block_rows
    outputs = lax.map(jax.checkpoint(attend_block), (queries.reshape(nblocks, block_rows, KVH, groups, AD), segment.reshape(nblocks, block_rows), position.reshape(nblocks, block_rows)))
    return outputs.reshape(length, QD)

def layer(signal, params, segment, position, alive_row):
    norm_gain, in_proj, conv_weight, conv_bias, gate_gain, out_proj, q_proj, kv_proj, o_proj, ff_gain, gate_up, down_proj, a_log, dt_bias, skip_scale = params
    length = signal.shape[0]
    normed = low(rms_scale(signal, norm_gain))
    mixed = low(low_back(product(normed, in_proj)))
    gate_input = mixed[:, :DI]
    xbc = mixed[:, DI:DI + XC]
    dt_raw = mixed[:, DI + XC:]
    activated = jax.nn.silu(causal_conv(xbc, conv_weight, conv_bias, position))
    values = activated[:, :DI].reshape(length, MH, HP)
    b_in = activated[:, DI:DI + NS]
    c_out = activated[:, DI + NS:]
    step_size = jax.nn.softplus(dt_raw + dt_bias[None, :])
    log_decay = -step_size * jnp.exp(a_log)[None, :]
    ssm_out = state_space(values, step_size, log_decay, b_in, c_out, segment, skip_scale).reshape(length, DI)
    mamba_norm = low(rms_scale(ssm_out * jax.nn.silu(gate_input), gate_gain))
    mamba_branch = low_back(product(mamba_norm, out_proj))
    queries = low(low_back(product(normed, q_proj)))
    keyvals = low(low_back(product(normed, kv_proj)))
    attended = low(low_back(attention(queries, keyvals, segment, position)))
    attn_branch = low_back(product(attended, o_proj))
    middle = signal + mamba_branch + attn_branch
    normed_ff = low(rms_scale(middle, ff_gain))
    gate_up_out = low(low_back(product(normed_ff, gate_up)))
    activation = low(jax.nn.silu(gate_up_out[:, :FF]) * gate_up_out[:, FF:])
    ff_branch = low_back(product(activation, down_proj))
    return (middle + ff_branch) * alive_row[:, None]

def reference(hidden, cotangent, seq_lengths, norm_gain, in_proj, conv_weight, conv_bias, gate_gain, out_proj, q_proj, kv_proj, o_proj, ff_gain, gate_up, down_proj, a_log, dt_bias, skip_scale):
    weights = tuple((weight.astype(jnp.float32) for weight in (norm_gain, in_proj, conv_weight, conv_bias, gate_gain, out_proj, q_proj, kv_proj, o_proj, ff_gain, gate_up, down_proj, a_log, dt_bias, skip_scale)))
    pair_count = MICRO * N_DP
    group_rows = N_CTX * TOK_DEV
    inputs = hidden.reshape(pair_count, N_CTX, TOK_DEV, D)
    cotans = cotangent.reshape(pair_count, N_CTX, TOK_DEV, D)
    spans = (jnp.transpose(seq_lengths, (1, 0, 2)).reshape(pair_count, SEQS) // N_CTX).astype(jnp.int32)

    def one_pair(totals, pair_items):
        block_x, block_ct, span_len = pair_items
        segment, offset, extent, start_row, alive_row = row_layout(span_len, TOK_DEV)
        places = jnp.arange(N_CTX, dtype=jnp.int32)[:, None]
        target = (N_CTX * start_row[None, :] + places * extent[None, :] + offset[None, :]).reshape(group_rows).astype(jnp.int32)
        position_dev = (places * extent[None, :] + offset[None, :]).reshape(group_rows).astype(jnp.int32)
        segment_dev = jnp.broadcast_to(segment[None, :], (N_CTX, TOK_DEV)).reshape(group_rows)
        alive_dev = jnp.broadcast_to(alive_row[None, :], (N_CTX, TOK_DEV)).reshape(group_rows)
        segment_ord = jnp.zeros((group_rows,), jnp.int32).at[target].set(segment_dev)
        position_ord = jnp.zeros((group_rows,), jnp.int32).at[target].set(position_dev)
        alive_ord = jnp.zeros((group_rows,), jnp.float32).at[target].set(alive_dev)
        x_ord = jnp.zeros((group_rows, D), jnp.float32).at[target].set(block_x.reshape(group_rows, D).astype(jnp.float32))
        ct_ord = jnp.zeros((group_rows, D), jnp.float32).at[target].set(block_ct.reshape(group_rows, D).astype(jnp.float32))

        def forward(x_value, *params):
            return layer(x_value, params, segment_ord, position_ord, alive_ord)
        result, pullback = jax.vjp(forward, x_ord, *weights)
        gradients = pullback(ct_ord)
        totals = tuple((total + grad for total, grad in zip(totals, gradients[1:])))
        return (totals, (result[target].reshape(N_CTX, TOK_DEV, D), gradients[0][target].reshape(N_CTX, TOK_DEV, D)))
    initial = tuple((jnp.zeros_like(weight) for weight in weights))
    totals, (outs, grads_x) = lax.scan(one_pair, initial, (inputs, cotans, spans))
    layer_out = outs.reshape(MICRO, TOKENS, D).astype(jnp.bfloat16)
    grad_hidden = grads_x.reshape(MICRO, TOKENS, D).astype(jnp.bfloat16)
    return (layer_out, grad_hidden, totals[0], totals[1], totals[2], totals[3], totals[4], totals[5], totals[6], totals[7], totals[8], totals[9], totals[10], totals[11], totals[12], totals[13], totals[14])
```

```python
import functools

import jax
import jax.numpy as jnp
from jax import lax
from jax.sharding import PartitionSpec as P

MH = 24
HP = 64
NS = 128
CONV = 4
AH = 8
KVH = 2
AD = 64
DI = 1536
XC = 1792
QD = 512
KD = 128


EPSILON = 1e-05
HIGHEST = lax.Precision.HIGHEST
MASKED = -1e30
EVERY = ("dp", "ctx")


def bit_list(count):
    bits = []
    size = 1
    while size < count:
        bits.append(size)
        size *= 2
    return bits


def swap_with(block, axes, count, bit):
    return lax.ppermute(block, axes, [(i, i ^ bit) for i in range(count)])


def spread(shard, axes, count, order):
    me = lax.axis_index(axes)
    held = shard[None]
    for bit in order:
        other = swap_with(held, axes, count, bit)
        upper = ((me // bit) % 2) == 1
        held = jnp.stack([jnp.where(upper, other, held), jnp.where(upper, held, other)])
    places = len(order)
    held = held.reshape((2,) * places + shard.shape)
    dims = order[::-1]
    turned = sorted(range(places), key=lambda k: -dims[k])
    held = held.transpose(tuple(turned) + tuple(range(places, places + shard.ndim)))
    return held.reshape((count,) + shard.shape)


def collect(parts, axes, count, order):
    me = lax.axis_index(axes)
    left = sorted(order, reverse=True)
    held = parts.reshape((2,) * len(order) + parts.shape[1:])
    for bit in order:
        at = left.index(bit)
        left.pop(at)
        upper = (me // bit) % 2
        kept = lax.dynamic_index_in_dim(held, upper, at, keepdims=False)
        sent = lax.dynamic_index_in_dim(held, 1 - upper, at, keepdims=False)
        other = swap_with(sent, axes, count, bit)
        held = (kept.astype(jnp.float32) + other.astype(jnp.float32)).astype(parts.dtype)
    return held


def sum_all(value, axes, count):
    for bit in bit_list(count):
        value = value + swap_with(value, axes, count, bit)
    return value


def chain_states(state, decay, axis, count, backward):
    me = lax.axis_index(axis)
    prefix = jnp.zeros_like(state)
    prefix_decay = jnp.ones_like(decay)
    total, total_decay = state, decay
    for bit in bit_list(count):
        other = swap_with(total.astype(jnp.bfloat16), axis, count, bit).astype(jnp.float32)
        other_decay = swap_with(total_decay, axis, count, bit)
        upper = ((me // bit) % 2) == 1
        later = jnp.logical_not(upper) if backward else upper
        prefix = jnp.where(later, prefix + prefix_decay * other, prefix)
        prefix_decay = jnp.where(later, prefix_decay * other_decay, prefix_decay)
        total = jnp.where(later, total + total_decay * other, other + other_decay * total)
        total_decay = total_decay * other_decay
    return prefix


def rms_scale(signal, scale):
    return signal * lax.rsqrt(jnp.mean(signal * signal, axis=-1, keepdims=True) + EPSILON) * scale


def swiglu(joined):
    half_cols = joined.shape[1] // 2
    return jax.nn.silu(joined[:, :half_cols]) * joined[:, half_cols:]


def plain_dot(first_arg, second_arg):
    return jnp.dot(first_arg, second_arg, preferred_element_type=jnp.float32)


def left_dot(first_arg, second_arg):
    return lax.dot_general(
        first_arg, second_arg, (((0,), (0,)), ((), ())), preferred_element_type=jnp.float32
    )


def right_dot(first_arg, second_arg):
    return lax.dot_general(
        first_arg, second_arg, (((1,), (1,)), ((), ())), preferred_element_type=jnp.float32
    )


def by_head(array):
    micro, rows, _ = array.shape
    return array.reshape(micro, rows, MH, HP).transpose(0, 2, 1, 3)


def mamba_local(xbc, raw_step, tail, w_conv, b_conv, log_a, bias_dt, skip_val, alive, allowed, offset):
    rows = xbc.shape[1]
    reach = CONV - 1
    longer = jnp.concatenate([tail, xbc], axis=1)
    convolved = b_conv + w_conv[reach] * xbc
    for shift_by in range(1, CONV):
        shifted = longer[:, reach - shift_by : reach - shift_by + rows]
        inside = alive | (offset >= shift_by)
        convolved = convolved + jnp.where(inside[..., None], shifted, 0.0) * w_conv[reach - shift_by]
    activated = jax.nn.silu(convolved)
    values = by_head(activated[..., :DI])
    b_in = activated[..., DI : DI + NS]
    c_out = activated[..., DI + NS :]
    step_size = jax.nn.softplus(raw_step + bias_dt).transpose(0, 2, 1)
    log_decay = -step_size * jnp.exp(log_a)[:, None]
    scaled = values * step_size[..., None]
    before = jnp.triu(jnp.ones((rows, rows), jnp.float32))
    within = jnp.einsum("mhs,st->mht", log_decay, before, precision=HIGHEST)
    live = alive.astype(jnp.float32)[:, None, :]
    span_sum = jnp.sum(log_decay * live, axis=-1, keepdims=True)
    inner_cb = jnp.einsum("mtn,msn->mts", c_out, b_in)
    gap = jnp.minimum(within[..., :, None] - within[..., None, :], 0.0)
    mixing = jnp.where(allowed[:, None], jnp.exp(gap), 0.0) * inner_cb[:, None]
    local_out = jnp.einsum("mhts,mhsp->mhtp", mixing, scaled) + skip_val[:, None, None] * values
    to_end = jnp.exp(jnp.minimum(span_sum - within, 0.0)) * live
    end_state = jnp.einsum("mhsp,msn->mhpn", scaled * to_end[..., None], b_in)
    from_start = jnp.exp(within) * live
    return (local_out, end_state, jnp.exp(span_sum), c_out, from_start)


def mamba_finish(local_out, c_out, from_start, state_in, gate_input, gate_scale):
    carried = jnp.einsum("mtn,mhpn->mhtp", c_out, state_in) * from_start[..., None]
    full_out = (local_out + carried).transpose(0, 2, 1, 3).reshape(gate_input.shape)
    return rms_scale(full_out * jax.nn.silu(gate_input), gate_scale)


def body(
    dp_count,
    ctx_count,
    hidden,
    cotangent,
    seq_lengths,
    norm_gain,
    in_proj,
    conv_weight,
    conv_bias,
    gate_gain,
    out_proj,
    q_proj,
    kv_proj,
    o_proj,
    ff_gain,
    gate_up,
    down_proj,
    a_log,
    dt_bias,
    skip_scale,
):
    count = dp_count * ctx_count
    ctx_place = lax.axis_index("ctx")
    micro, rows, width = hidden.shape
    all_rows = micro * rows
    groups = AH // KVH
    scale_qk = AD ** (-0.5)
    bits = bit_list(count)
    order_a = bits[::-1]
    order_b = list(order_a)
    if count == 32:
        order_a = [16, 8, 4, 2, 1]
        order_b = [16, 8, 2, 4, 1]

    small_parts = (norm_gain, conv_weight.reshape(-1), conv_bias, gate_gain, ff_gain)
    small_sizes = [part.shape[0] for part in small_parts]
    small_width = -(-sum(small_sizes) // 128) * 128
    pad = small_width - sum(small_sizes)
    small_shard = jnp.concatenate(small_parts + (jnp.zeros((pad,), jnp.bfloat16),))
    small_all = spread(small_shard.reshape(-1, 128), EVERY, count, order_a).reshape(count, -1)
    cut = [0]
    for size in small_sizes:
        cut.append(cut[-1] + size)
    g_norm = small_all[:, cut[0] : cut[1]].reshape(-1).astype(jnp.float32)
    w_conv = (
        small_all[:, cut[1] : cut[2]]
        .reshape(count, CONV, -1)
        .transpose(1, 0, 2)
        .reshape(CONV, -1)
        .astype(jnp.float32)
    )
    b_conv = small_all[:, cut[2] : cut[3]].reshape(-1).astype(jnp.float32)
    g_gate = small_all[:, cut[3] : cut[4]].reshape(-1).astype(jnp.float32)
    g_ff = small_all[:, cut[4] : cut[5]].reshape(-1).astype(jnp.float32)

    front_shard = jnp.concatenate([q_proj, kv_proj, in_proj], axis=1)
    halfway = front_shard.shape[0] // 2
    front_low = spread(front_shard[:halfway], EVERY, count, order_a)
    front_high = spread(front_shard[halfway:], EVERY, count, order_b)
    w_front = jnp.concatenate([front_low, front_high], axis=1).reshape(width, -1)
    close_shard = jnp.concatenate([out_proj, o_proj], axis=0)
    close_all = spread(close_shard, EVERY, count, order_b)
    out_rows = out_proj.shape[0]
    w_out = close_all[:, :out_rows].reshape(-1, width)
    w_o = close_all[:, out_rows:].reshape(-1, width)
    w_gu = spread(gate_up, EVERY, count, order_a).reshape(width, -1)
    w_down = spread(down_proj, EVERY, count, order_b).reshape(-1, width)

    span_len = seq_lengths[0, :, 0] // ctx_count
    local_row = jnp.arange(rows, dtype=jnp.int32)[None, :]
    alive = local_row < span_len[:, None]
    offset = jnp.where(alive, local_row, local_row - span_len[:, None])
    extent = jnp.where(alive, span_len[:, None], rows - span_len[:, None])
    position = ctx_place * extent + offset
    same = alive[:, :, None] == alive[:, None, :]
    causal = local_row[0][:, None] >= local_row[0][None, :]
    alive_row = alive.reshape(-1, 1).astype(jnp.float32)

    x_in = hidden.reshape(all_rows, width).astype(jnp.float32)
    normed, norm_pull = jax.vjp(rms_scale, x_in, g_norm)
    normed_b = normed.astype(jnp.bfloat16)
    joined = plain_dot(normed_b, w_front).astype(jnp.bfloat16)
    query_b = joined[:, :QD]
    keyval_b = joined[:, QD : QD + 2 * KD]
    mixed = joined[:, QD + 2 * KD :]
    gate_z = mixed[:, :DI].astype(jnp.float32).reshape(micro, rows, DI)
    xbc_b = mixed[:, DI : DI + XC].reshape(micro, rows, XC)
    raw_step = mixed[:, DI + XC :].astype(jnp.float32).reshape(micro, rows, MH)

    reach = CONV - 1
    tail_rows = jnp.stack(
        [
            lax.dynamic_slice_in_dim(xbc_b[index], span_len[index] - reach, reach, 0)
            for index in range(micro)
        ]
    )
    tail_in = lax.ppermute(tail_rows, "ctx", [(i, i + 1) for i in range(ctx_count - 1)])
    ctx_order = bit_list(ctx_count)[::-1]
    every_kv = spread(keyval_b.reshape(micro, rows, 2 * KD), "ctx", ctx_count, ctx_order)

    def mamba_front(*args):
        return mamba_local(*args, alive, same & causal, offset)

    front_out, front_pull = jax.vjp(
        mamba_front,
        xbc_b.astype(jnp.float32),
        raw_step,
        tail_in.astype(jnp.float32),
        w_conv,
        b_conv,
        a_log,
        dt_bias,
        skip_scale,
    )
    local_out, end_state, span_decay, c_out, from_start = front_out
    decay_wide = span_decay[..., None]
    state_in = chain_states(end_state, decay_wide, "ctx", ctx_count, False)

    query_heads = query_b.reshape(micro, rows, KVH, groups, AD).transpose(0, 2, 3, 1, 4)
    key_heads = every_kv[..., :KD].reshape(ctx_count, micro, rows, KVH, AD).transpose(1, 3, 0, 2, 4)
    key_heads = key_heads.reshape(micro, KVH, ctx_count * rows, AD)
    value_heads = every_kv[..., KD:].reshape(ctx_count, micro, rows, KVH, AD)
    value_heads = value_heads.transpose(1, 3, 0, 2, 4).reshape(micro, KVH, ctx_count * rows, AD)
    source = jnp.arange(ctx_count, dtype=jnp.int32)[None, :, None]
    key_pos = (source * extent[:, None, :] + offset[:, None, :]).reshape(micro, -1)
    key_alive = jnp.broadcast_to(alive[:, None, :], (micro, ctx_count, rows)).reshape(micro, -1)
    seen = (alive[:, :, None] == key_alive[:, None, :]) & (
        position[:, :, None] >= key_pos[:, None, :]
    )
    seen = seen[:, None, None]
    scores = (
        jnp.einsum("mgjtd,mgsd->mgjts", query_heads, key_heads, preferred_element_type=jnp.float32)
        * scale_qk
    )
    scores = jnp.where(seen, scores, MASKED)
    weights = jnp.exp(scores - jnp.max(scores, axis=-1, keepdims=True))
    probs = weights / jnp.sum(weights, axis=-1, keepdims=True)
    probs_b = probs.astype(jnp.bfloat16)
    attended = jnp.einsum(
        "mgjts,mgsd->mgjtd", probs_b, value_heads, preferred_element_type=jnp.float32
    )
    attended_b = attended.transpose(0, 3, 1, 2, 4).reshape(all_rows, QD).astype(jnp.bfloat16)
    attn_branch = plain_dot(attended_b, w_o)

    mamba_norm, finish_pull = jax.vjp(
        mamba_finish, local_out, c_out, from_start, state_in, gate_z, g_gate
    )
    mamba_norm_b = mamba_norm.reshape(all_rows, DI).astype(jnp.bfloat16)
    middle = x_in + plain_dot(mamba_norm_b, w_out) + attn_branch
    normed_ff, ff_pull = jax.vjp(rms_scale, middle, g_ff)
    normed_ff_b = normed_ff.astype(jnp.bfloat16)
    gate_up_b = plain_dot(normed_ff_b, w_gu).astype(jnp.bfloat16)
    activation, act_pull = jax.vjp(swiglu, gate_up_b.astype(jnp.float32))
    activation_b = activation.astype(jnp.bfloat16)
    layer_out = ((middle + plain_dot(activation_b, w_down)) * alive_row).astype(jnp.bfloat16)

    def owned(grad, order):
        return collect(grad.reshape((count, -1) + grad.shape[1:]), EVERY, count, order)

    back_a = order_a[::-1]
    back_b = order_b[::-1]
    d_out = cotangent.reshape(all_rows, width).astype(jnp.float32) * alive_row
    d_ff_b = d_out.astype(jnp.bfloat16)
    r_down = owned(left_dot(activation_b, d_ff_b).astype(jnp.bfloat16), back_b)
    (d_gate_up,) = act_pull(right_dot(d_ff_b, w_down))
    d_gate_up_b = d_gate_up.astype(jnp.bfloat16)
    r_gu = owned(left_dot(normed_ff_b, d_gate_up_b).astype(jnp.bfloat16), back_a)
    d_mid_part, g_ffgain = ff_pull(right_dot(d_gate_up_b, w_gu))
    d_mid = d_out + d_mid_part
    d_branch_b = d_mid.astype(jnp.bfloat16)
    d_mamba_norm = right_dot(d_branch_b, w_out).reshape(micro, rows, DI)
    d_local, d_cout, d_from, d_state_in, d_gate_z, g_gategain = finish_pull(d_mamba_norm)
    d_end_state = chain_states(d_state_in, decay_wide, "ctx", ctx_count, True)
    g_close = jnp.concatenate(
        [
            left_dot(mamba_norm_b, d_branch_b).astype(jnp.bfloat16).reshape(count, -1, width),
            left_dot(attended_b, d_branch_b).astype(jnp.bfloat16).reshape(count, -1, width),
        ],
        axis=1,
    )
    r_close = collect(g_close, EVERY, count, back_b)

    d_attended_b = right_dot(d_branch_b, w_o).astype(jnp.bfloat16)
    d_att_heads = d_attended_b.reshape(micro, rows, KVH, groups, AD).transpose(0, 2, 3, 1, 4)
    d_probs = jnp.einsum(
        "mgjtd,mgsd->mgjts", d_att_heads, value_heads, preferred_element_type=jnp.float32
    )
    row_delta = jnp.sum(d_att_heads.astype(jnp.float32) * attended, axis=-1, keepdims=True)
    d_score = (probs * (d_probs - row_delta)).astype(jnp.bfloat16)
    d_query = jnp.einsum(
        "mgjts,mgsd->mtgjd", d_score, key_heads, preferred_element_type=jnp.float32
    )
    d_query_b = (d_query * scale_qk).reshape(all_rows, QD).astype(jnp.bfloat16)
    d_keys = jnp.einsum(
        "mgjts,mgjtd->msgd", d_score, query_heads, preferred_element_type=jnp.float32
    )
    d_values = jnp.einsum(
        "mgjts,mgjtd->msgd", probs_b, d_att_heads, preferred_element_type=jnp.float32
    )
    d_kv_parts = jnp.concatenate(
        [
            (d_keys * scale_qk).reshape(micro, ctx_count, rows, KD),
            d_values.reshape(micro, ctx_count, rows, KD),
        ],
        axis=-1,
    ).transpose(1, 0, 2, 3)
    d_keyval = collect(d_kv_parts.astype(jnp.bfloat16), "ctx", ctx_count, ctx_order[::-1])
    d_keyval = d_keyval.reshape(all_rows, 2 * KD)

    d_span_decay = jnp.sum(d_end_state * state_in, axis=(2, 3))[..., None]
    d_xbc, d_raw_step, d_tail, g_conv, g_convbias, g_alog, g_dtbias, g_skip = front_pull(
        (d_local, d_end_state, d_span_decay, d_cout, d_from)
    )
    tail_back = lax.ppermute(d_tail, "ctx", [(i + 1, i) for i in range(ctx_count - 1)])
    row_index = jnp.arange(rows, dtype=jnp.int32)[None, :]
    for step in range(reach):
        hit = row_index == (span_len[:, None] - reach + step)
        d_xbc = d_xbc + jnp.where(hit[..., None], tail_back[:, step : step + 1], 0.0)
    d_joined_b = jnp.concatenate(
        [
            d_query_b,
            d_keyval,
            d_gate_z.reshape(all_rows, DI).astype(jnp.bfloat16),
            d_xbc.reshape(all_rows, XC).astype(jnp.bfloat16),
            d_raw_step.reshape(all_rows, MH).astype(jnp.bfloat16),
        ],
        axis=1,
    )
    g_front = left_dot(normed_b, d_joined_b).astype(jnp.bfloat16)
    g_front = g_front.reshape((count, 2, halfway, -1))
    r_front = jnp.concatenate(
        [collect(g_front[:, 0], EVERY, count, back_a), collect(g_front[:, 1], EVERY, count, back_b)],
        axis=0,
    ).astype(jnp.float32)
    d_x_part, g_normgain = norm_pull(right_dot(d_joined_b, w_front))
    grad_hidden = (d_mid + d_x_part).astype(jnp.bfloat16)

    small_grads = jnp.concatenate(
        [
            g_normgain.reshape(count, -1),
            g_conv.reshape(CONV, count, -1).transpose(1, 0, 2).reshape(count, -1),
            g_convbias.reshape(count, -1),
            g_gategain.reshape(count, -1),
            g_ffgain.reshape(count, -1),
            jnp.zeros((count, pad), jnp.float32),
        ],
        axis=1,
    ).reshape(count, -1, 128)
    r_small = collect(small_grads, EVERY, count, back_a).reshape(-1)
    heads = jnp.concatenate([g_alog, g_dtbias, g_skip, jnp.zeros((128 - 3 * MH,), jnp.float32)])
    heads = sum_all(heads.reshape(1, 128), EVERY, count)[0]
    own = [r_small[cut[k] : cut[k + 1]] for k in range(5)]
    r_close = r_close.astype(jnp.float32)
    return (
        layer_out.reshape(hidden.shape),
        grad_hidden.reshape(hidden.shape),
        own[0],
        r_front[:, QD + 2 * KD :],
        own[1].reshape(CONV, -1),
        own[2],
        own[3],
        r_close[:out_rows],
        r_front[:, :QD],
        r_front[:, QD : QD + 2 * KD],
        r_close[out_rows:],
        own[4],
        r_gu.astype(jnp.float32),
        r_down.astype(jnp.float32),
        heads[:MH],
        heads[MH : 2 * MH],
        heads[2 * MH : 3 * MH],
    )


def solution(mesh):
    placed = (
        P(None, ("dp", "ctx"), None),
        P(None, ("dp", "ctx"), None),
        P("dp", None, None),
        P(("dp", "ctx")),
        P(("dp", "ctx"), None),
        P(None, ("dp", "ctx")),
        P(("dp", "ctx")),
        P(("dp", "ctx")),
        P(("dp", "ctx"), None),
        P(("dp", "ctx"), None),
        P(("dp", "ctx"), None),
        P(("dp", "ctx"), None),
        P(("dp", "ctx")),
        P(("dp", "ctx"), None),
        P(("dp", "ctx"), None),
        P(),
        P(),
        P(),
    )
    return jax.shard_map(
        functools.partial(body, mesh.shape["dp"], mesh.shape["ctx"]),
        mesh=mesh,
        in_specs=placed,
        out_specs=(
            P(None, ("dp", "ctx"), None),
            P(None, ("dp", "ctx"), None),
            P(("dp", "ctx")),
            P(("dp", "ctx"), None),
            P(None, ("dp", "ctx")),
            P(("dp", "ctx")),
            P(("dp", "ctx")),
            P(("dp", "ctx"), None),
            P(("dp", "ctx"), None),
            P(("dp", "ctx"), None),
            P(("dp", "ctx"), None),
            P(("dp", "ctx")),
            P(("dp", "ctx"), None),
            P(("dp", "ctx"), None),
            P(),
            P(),
            P(),
        ),
        check_vma=False,
    )
```

```python
import functools

import jax
import jax.numpy as jnp
from jax import lax
from jax.sharding import PartitionSpec as P

MH = 24
HP = 64
NS = 128
CONV = 4
AH = 8
KVH = 2
AD = 64
DI = 1536
XC = 1792
QD = 512
KD = 128


EPSILON = 1e-05
HIGHEST = lax.Precision.HIGHEST
MASKED = -1e30
EVERY = ("dp", "ctx")


def bit_list(count):
    bits = []
    size = 1
    while size < count:
        bits.append(size)
        size *= 2
    return bits


def swap_with(block, axes, count, bit):
    return lax.ppermute(block, axes, [(i, i ^ bit) for i in range(count)])


def spread(shard, axes, count, order):
    me = lax.axis_index(axes)
    held = shard[None]
    for bit in order:
        other = swap_with(held, axes, count, bit)
        upper = ((me // bit) % 2) == 1
        held = jnp.stack([jnp.where(upper, other, held), jnp.where(upper, held, other)])
    places = len(order)
    held = held.reshape((2,) * places + shard.shape)
    dims = order[::-1]
    turned = sorted(range(places), key=lambda k: -dims[k])
    held = held.transpose(tuple(turned) + tuple(range(places, places + shard.ndim)))
    return held.reshape((count,) + shard.shape)


def collect(parts, axes, count, order):
    me = lax.axis_index(axes)
    left = sorted(order, reverse=True)
    held = parts.reshape((2,) * len(order) + parts.shape[1:])
    for bit in order:
        at = left.index(bit)
        left.pop(at)
        upper = (me // bit) % 2
        kept = lax.dynamic_index_in_dim(held, upper, at, keepdims=False)
        sent = lax.dynamic_index_in_dim(held, 1 - upper, at, keepdims=False)
        other = swap_with(sent, axes, count, bit)
        held = (kept.astype(jnp.float32) + other.astype(jnp.float32)).astype(parts.dtype)
    return held


def sum_all(value, axes, count):
    for bit in bit_list(count):
        value = value + swap_with(value, axes, count, bit)
    return value


def chain_states(state, decay, axis, count, backward):
    me = lax.axis_index(axis)
    prefix = jnp.zeros_like(state)
    prefix_decay = jnp.ones_like(decay)
    total, total_decay = state, decay
    for bit in bit_list(count):
        other = swap_with(total.astype(jnp.bfloat16), axis, count, bit).astype(jnp.float32)
        other_decay = swap_with(total_decay, axis, count, bit)
        upper = ((me // bit) % 2) == 1
        later = jnp.logical_not(upper) if backward else upper
        prefix = jnp.where(later, prefix + prefix_decay * other, prefix)
        prefix_decay = jnp.where(later, prefix_decay * other_decay, prefix_decay)
        total = jnp.where(later, total + total_decay * other, other + other_decay * total)
        total_decay = total_decay * other_decay
    return prefix


def rms_scale(signal, scale):
    return signal * lax.rsqrt(jnp.mean(signal * signal, axis=-1, keepdims=True) + EPSILON) * scale


def swiglu(joined):
    half_cols = joined.shape[1] // 2
    return jax.nn.silu(joined[:, :half_cols]) * joined[:, half_cols:]


def plain_dot(first_arg, second_arg):
    return jnp.dot(first_arg, second_arg, preferred_element_type=jnp.float32)


def left_dot(first_arg, second_arg):
    return lax.dot_general(
        first_arg, second_arg, (((0,), (0,)), ((), ())), preferred_element_type=jnp.float32
    )


def right_dot(first_arg, second_arg):
    return lax.dot_general(
        first_arg, second_arg, (((1,), (1,)), ((), ())), preferred_element_type=jnp.float32
    )


def by_head(array):
    micro, rows, _ = array.shape
    return array.reshape(micro, rows, MH, HP).transpose(0, 2, 1, 3)


def mamba_local(xbc, raw_step, tail, w_conv, b_conv, log_a, bias_dt, skip_val, alive, allowed, offset):
    rows = xbc.shape[1]
    reach = CONV - 1
    longer = jnp.concatenate([tail, xbc], axis=1)
    convolved = b_conv + w_conv[reach] * xbc
    for shift_by in range(1, CONV):
        shifted = longer[:, reach - shift_by : reach - shift_by + rows]
        inside = alive | (offset >= shift_by)
        convolved = convolved + jnp.where(inside[..., None], shifted, 0.0) * w_conv[reach - shift_by]
    activated = jax.nn.silu(convolved)
    values = by_head(activated[..., :DI])
    b_in = activated[..., DI : DI + NS]
    c_out = activated[..., DI + NS :]
    step_size = jax.nn.softplus(raw_step + bias_dt).transpose(0, 2, 1)
    log_decay = -step_size * jnp.exp(log_a)[:, None]
    scaled = values * step_size[..., None]
    before = jnp.triu(jnp.ones((rows, rows), jnp.float32))
    within = jnp.einsum("mhs,st->mht", log_decay, before, precision=HIGHEST)
    live = alive.astype(jnp.float32)[:, None, :]
    span_sum = jnp.sum(log_decay * live, axis=-1, keepdims=True)
    inner_cb = jnp.einsum("mtn,msn->mts", c_out, b_in)
    gap = jnp.minimum(within[..., :, None] - within[..., None, :], 0.0)
    mixing = jnp.where(allowed[:, None], jnp.exp(gap), 0.0) * inner_cb[:, None]
    local_out = jnp.einsum("mhts,mhsp->mhtp", mixing, scaled) + skip_val[:, None, None] * values
    to_end = jnp.exp(jnp.minimum(span_sum - within, 0.0)) * live
    end_state = jnp.einsum("mhsp,msn->mhpn", scaled * to_end[..., None], b_in)
    from_start = jnp.exp(within) * live
    return (local_out, end_state, jnp.exp(span_sum), c_out, from_start)


def mamba_finish(local_out, c_out, from_start, state_in, gate_input, gate_scale):
    carried = jnp.einsum("mtn,mhpn->mhtp", c_out, state_in) * from_start[..., None]
    full_out = (local_out + carried).transpose(0, 2, 1, 3).reshape(gate_input.shape)
    return rms_scale(full_out * jax.nn.silu(gate_input), gate_scale)


def body(
    dp_count,
    ctx_count,
    hidden,
    cotangent,
    seq_lengths,
    norm_gain,
    in_proj,
    conv_weight,
    conv_bias,
    gate_gain,
    out_proj,
    q_proj,
    kv_proj,
    o_proj,
    ff_gain,
    gate_up,
    down_proj,
    a_log,
    dt_bias,
    skip_scale,
):
    count = dp_count * ctx_count
    ctx_place = lax.axis_index("ctx")
    micro, rows, width = hidden.shape
    all_rows = micro * rows
    groups = AH // KVH
    scale_qk = AD ** (-0.5)
    bits = bit_list(count)
    order_a = bits[::-1]
    order_b = list(order_a)
    if count == 32:
        order_a = [16, 8, 4, 2, 1]
        order_b = [16, 8, 2, 4, 1]

    small_parts = (norm_gain, conv_weight.reshape(-1), conv_bias, gate_gain, ff_gain)
    small_sizes = [part.shape[0] for part in small_parts]
    small_width = -(-sum(small_sizes) // 128) * 128
    pad = small_width - sum(small_sizes)
    small_shard = jnp.concatenate(small_parts + (jnp.zeros((pad,), jnp.bfloat16),))
    small_all = spread(small_shard.reshape(-1, 128), EVERY, count, order_a).reshape(count, -1)
    cut = [0]
    for size in small_sizes:
        cut.append(cut[-1] + size)
    g_norm = small_all[:, cut[0] : cut[1]].reshape(-1).astype(jnp.float32)
    w_conv = (
        small_all[:, cut[1] : cut[2]]
        .reshape(count, CONV, -1)
        .transpose(1, 0, 2)
        .reshape(CONV, -1)
        .astype(jnp.float32)
    )
    b_conv = small_all[:, cut[2] : cut[3]].reshape(-1).astype(jnp.float32)
    g_gate = small_all[:, cut[3] : cut[4]].reshape(-1).astype(jnp.float32)
    g_ff = small_all[:, cut[4] : cut[5]].reshape(-1).astype(jnp.float32)

    def gather(shard, after):
        if after is not None:
            shard = shard + after[:1, :1] * 0
        return lax.all_gather(shard, EVERY, axis=0, tiled=True)

    out_rows = out_proj.shape[0]
    both_rows = out_rows + o_proj.shape[0]
    w_front = gather(jnp.concatenate([q_proj, kv_proj, in_proj], axis=1), None)
    tall = gather(jnp.concatenate([out_proj, o_proj, down_proj], axis=0), w_front)
    w_gu = gather(gate_up, tall)
    tall = tall.reshape(count, -1, width)
    w_out = tall[:, :out_rows].reshape(-1, width)
    w_o = tall[:, out_rows:both_rows].reshape(-1, width)
    w_down = tall[:, both_rows:].reshape(-1, width)

    span_len = seq_lengths[0, :, 0] // ctx_count
    local_row = jnp.arange(rows, dtype=jnp.int32)[None, :]
    alive = local_row < span_len[:, None]
    offset = jnp.where(alive, local_row, local_row - span_len[:, None])
    extent = jnp.where(alive, span_len[:, None], rows - span_len[:, None])
    position = ctx_place * extent + offset
    same = alive[:, :, None] == alive[:, None, :]
    causal = local_row[0][:, None] >= local_row[0][None, :]
    alive_row = alive.reshape(-1, 1).astype(jnp.float32)

    x_in = hidden.reshape(all_rows, width).astype(jnp.float32)
    normed, norm_pull = jax.vjp(rms_scale, x_in, g_norm)
    normed_b = normed.astype(jnp.bfloat16)
    joined = plain_dot(normed_b, w_front).astype(jnp.bfloat16)
    query_b = joined[:, :QD]
    keyval_b = joined[:, QD : QD + 2 * KD]
    mixed = joined[:, QD + 2 * KD :]
    gate_z = mixed[:, :DI].astype(jnp.float32).reshape(micro, rows, DI)
    xbc_b = mixed[:, DI : DI + XC].reshape(micro, rows, XC)
    raw_step = mixed[:, DI + XC :].astype(jnp.float32).reshape(micro, rows, MH)

    reach = CONV - 1
    tail_rows = jnp.stack(
        [
            lax.dynamic_slice_in_dim(xbc_b[index], span_len[index] - reach, reach, 0)
            for index in range(micro)
        ]
    )
    tail_in = lax.ppermute(tail_rows, "ctx", [(i, i + 1) for i in range(ctx_count - 1)])
    ctx_order = bit_list(ctx_count)[::-1]
    every_kv = spread(keyval_b.reshape(micro, rows, 2 * KD), "ctx", ctx_count, ctx_order)

    def mamba_front(*args):
        return mamba_local(*args, alive, same & causal, offset)

    front_out, front_pull = jax.vjp(
        mamba_front,
        xbc_b.astype(jnp.float32),
        raw_step,
        tail_in.astype(jnp.float32),
        w_conv,
        b_conv,
        a_log,
        dt_bias,
        skip_scale,
    )
    local_out, end_state, span_decay, c_out, from_start = front_out
    decay_wide = span_decay[..., None]
    state_in = chain_states(end_state, decay_wide, "ctx", ctx_count, False)

    query_heads = query_b.reshape(micro, rows, KVH, groups, AD).transpose(0, 2, 3, 1, 4)
    key_heads = every_kv[..., :KD].reshape(ctx_count, micro, rows, KVH, AD).transpose(1, 3, 0, 2, 4)
    key_heads = key_heads.reshape(micro, KVH, ctx_count * rows, AD)
    value_heads = every_kv[..., KD:].reshape(ctx_count, micro, rows, KVH, AD)
    value_heads = value_heads.transpose(1, 3, 0, 2, 4).reshape(micro, KVH, ctx_count * rows, AD)
    source = jnp.arange(ctx_count, dtype=jnp.int32)[None, :, None]
    key_pos = (source * extent[:, None, :] + offset[:, None, :]).reshape(micro, -1)
    key_alive = jnp.broadcast_to(alive[:, None, :], (micro, ctx_count, rows)).reshape(micro, -1)
    seen = (alive[:, :, None] == key_alive[:, None, :]) & (
        position[:, :, None] >= key_pos[:, None, :]
    )
    seen = seen[:, None, None]
    scores = (
        jnp.einsum("mgjtd,mgsd->mgjts", query_heads, key_heads, preferred_element_type=jnp.float32)
        * scale_qk
    )
    scores = jnp.where(seen, scores, MASKED)
    weights = jnp.exp(scores - jnp.max(scores, axis=-1, keepdims=True))
    probs = weights / jnp.sum(weights, axis=-1, keepdims=True)
    probs_b = probs.astype(jnp.bfloat16)
    attended = jnp.einsum(
        "mgjts,mgsd->mgjtd", probs_b, value_heads, preferred_element_type=jnp.float32
    )
    attended_b = attended.transpose(0, 3, 1, 2, 4).reshape(all_rows, QD).astype(jnp.bfloat16)
    attn_branch = plain_dot(attended_b, w_o)

    mamba_norm, finish_pull = jax.vjp(
        mamba_finish, local_out, c_out, from_start, state_in, gate_z, g_gate
    )
    mamba_norm_b = mamba_norm.reshape(all_rows, DI).astype(jnp.bfloat16)
    middle = x_in + plain_dot(mamba_norm_b, w_out) + attn_branch
    normed_ff, ff_pull = jax.vjp(rms_scale, middle, g_ff)
    normed_ff_b = normed_ff.astype(jnp.bfloat16)
    gate_up_b = plain_dot(normed_ff_b, w_gu).astype(jnp.bfloat16)
    activation, act_pull = jax.vjp(swiglu, gate_up_b.astype(jnp.float32))
    activation_b = activation.astype(jnp.bfloat16)
    layer_out = ((middle + plain_dot(activation_b, w_down)) * alive_row).astype(jnp.bfloat16)

    def owned(grad, order):
        grad = grad.astype(jnp.bfloat16).reshape((count, -1) + grad.shape[1:])
        return collect(grad, EVERY, count, order).astype(jnp.float32)

    back_a = order_a[::-1]
    back_b = order_b[::-1]
    d_out = cotangent.reshape(all_rows, width).astype(jnp.float32) * alive_row
    d_ff_b = d_out.astype(jnp.bfloat16)
    g_down = left_dot(activation_b, d_ff_b).astype(jnp.bfloat16)
    (d_gate_up,) = act_pull(right_dot(d_ff_b, w_down))
    d_gate_up_b = d_gate_up.astype(jnp.bfloat16)
    g_gu = [
        left_dot(normed_ff_b, d_gate_up_b[:, start : start + width]).astype(jnp.bfloat16)
        for start in range(0, d_gate_up_b.shape[1], width)
    ]
    d_mid_part, g_ffgain = ff_pull(right_dot(d_gate_up_b, w_gu))
    d_mid = d_out + d_mid_part
    d_branch_b = d_mid.astype(jnp.bfloat16)
    d_mamba_norm = right_dot(d_branch_b, w_out).reshape(micro, rows, DI)
    d_local, d_cout, d_from, d_state_in, d_gate_z, g_gategain = finish_pull(d_mamba_norm)
    d_end_state = chain_states(d_state_in, decay_wide, "ctx", ctx_count, True)
    tall_grads = g_gu + [
        left_dot(mamba_norm_b, d_branch_b).astype(jnp.bfloat16),
        left_dot(attended_b, d_branch_b).astype(jnp.bfloat16),
        g_down,
    ]
    tall_grads = [grad.reshape(count, -1, width) for grad in tall_grads]
    r_tall = lax.psum_scatter(
        jnp.concatenate(tall_grads, axis=1).reshape(-1, width),
        EVERY,
        scatter_dimension=0,
        tiled=True,
    ).astype(jnp.float32)
    gu_rows = gate_up.shape[0]
    after_gu = gu_rows * len(g_gu)
    r_gu = jnp.concatenate(
        [r_tall[k * gu_rows : (k + 1) * gu_rows] for k in range(len(g_gu))], axis=1
    )
    r_out = r_tall[after_gu : after_gu + out_rows]
    r_o = r_tall[after_gu + out_rows : after_gu + both_rows]
    r_down = r_tall[after_gu + both_rows :]

    d_attended_b = right_dot(d_branch_b, w_o).astype(jnp.bfloat16)
    d_att_heads = d_attended_b.reshape(micro, rows, KVH, groups, AD).transpose(0, 2, 3, 1, 4)
    d_probs = jnp.einsum(
        "mgjtd,mgsd->mgjts", d_att_heads, value_heads, preferred_element_type=jnp.float32
    )
    row_delta = jnp.sum(d_att_heads.astype(jnp.float32) * attended, axis=-1, keepdims=True)
    d_score = (probs * (d_probs - row_delta)).astype(jnp.bfloat16)
    d_query = jnp.einsum(
        "mgjts,mgsd->mtgjd", d_score, key_heads, preferred_element_type=jnp.float32
    )
    d_query_b = (d_query * scale_qk).reshape(all_rows, QD).astype(jnp.bfloat16)
    d_keys = jnp.einsum(
        "mgjts,mgjtd->msgd", d_score, query_heads, preferred_element_type=jnp.float32
    )
    d_values = jnp.einsum(
        "mgjts,mgjtd->msgd", probs_b, d_att_heads, preferred_element_type=jnp.float32
    )
    d_kv_parts = jnp.concatenate(
        [
            (d_keys * scale_qk).reshape(micro, ctx_count, rows, KD),
            d_values.reshape(micro, ctx_count, rows, KD),
        ],
        axis=-1,
    ).transpose(1, 0, 2, 3)
    d_keyval = collect(d_kv_parts.astype(jnp.bfloat16), "ctx", ctx_count, ctx_order[::-1])
    d_keyval = d_keyval.reshape(all_rows, 2 * KD)

    d_span_decay = jnp.sum(d_end_state * state_in, axis=(2, 3))[..., None]
    d_xbc, d_raw_step, d_tail, g_conv, g_convbias, g_alog, g_dtbias, g_skip = front_pull(
        (d_local, d_end_state, d_span_decay, d_cout, d_from)
    )
    tail_back = lax.ppermute(d_tail, "ctx", [(i + 1, i) for i in range(ctx_count - 1)])
    row_index = jnp.arange(rows, dtype=jnp.int32)[None, :]
    for step in range(reach):
        hit = row_index == (span_len[:, None] - reach + step)
        d_xbc = d_xbc + jnp.where(hit[..., None], tail_back[:, step : step + 1], 0.0)
    d_early_b = jnp.concatenate(
        [d_query_b, d_keyval, d_gate_z.reshape(all_rows, DI).astype(jnp.bfloat16)], axis=1
    )
    d_late_b = jnp.concatenate(
        [
            d_xbc.reshape(all_rows, XC).astype(jnp.bfloat16),
            d_raw_step.reshape(all_rows, MH).astype(jnp.bfloat16),
        ],
        axis=1,
    )
    half_late = XC // 2
    r_early = owned(left_dot(normed_b, d_early_b), back_b)
    r_late_a = owned(left_dot(normed_b, d_late_b[:, :half_late]), back_a)
    r_late_b = owned(left_dot(normed_b, d_late_b[:, half_late:]), back_b)
    r_front = jnp.concatenate([r_early, r_late_a, r_late_b], axis=1)
    d_joined_b = jnp.concatenate([d_early_b, d_late_b], axis=1)
    d_x_part, g_normgain = norm_pull(right_dot(d_joined_b, w_front))
    grad_hidden = (d_mid + d_x_part).astype(jnp.bfloat16)

    small_grads = jnp.concatenate(
        [
            g_normgain.reshape(count, -1),
            g_conv.reshape(CONV, count, -1).transpose(1, 0, 2).reshape(count, -1),
            g_convbias.reshape(count, -1),
            g_gategain.reshape(count, -1),
            g_ffgain.reshape(count, -1),
            jnp.zeros((count, pad), jnp.float32),
        ],
        axis=1,
    ).reshape(count, -1, 128)
    r_small = collect(small_grads, EVERY, count, back_a).reshape(-1)
    heads = jnp.concatenate([g_alog, g_dtbias, g_skip, jnp.zeros((128 - 3 * MH,), jnp.float32)])
    heads = sum_all(heads.reshape(1, 128), EVERY, count)[0]
    own = [r_small[cut[k] : cut[k + 1]] for k in range(5)]
    return (
        layer_out.reshape(hidden.shape),
        grad_hidden.reshape(hidden.shape),
        own[0],
        r_front[:, QD + 2 * KD :],
        own[1].reshape(CONV, -1),
        own[2],
        own[3],
        r_out,
        r_front[:, :QD],
        r_front[:, QD : QD + 2 * KD],
        r_o,
        own[4],
        r_gu,
        r_down,
        heads[:MH],
        heads[MH : 2 * MH],
        heads[2 * MH : 3 * MH],
    )


def solution(mesh):
    placed = (
        P(None, ("dp", "ctx"), None),
        P(None, ("dp", "ctx"), None),
        P("dp", None, None),
        P(("dp", "ctx")),
        P(("dp", "ctx"), None),
        P(None, ("dp", "ctx")),
        P(("dp", "ctx")),
        P(("dp", "ctx")),
        P(("dp", "ctx"), None),
        P(("dp", "ctx"), None),
        P(("dp", "ctx"), None),
        P(("dp", "ctx"), None),
        P(("dp", "ctx")),
        P(("dp", "ctx"), None),
        P(("dp", "ctx"), None),
        P(),
        P(),
        P(),
    )
    return jax.shard_map(
        functools.partial(body, mesh.shape["dp"], mesh.shape["ctx"]),
        mesh=mesh,
        in_specs=placed,
        out_specs=(
            P(None, ("dp", "ctx"), None),
            P(None, ("dp", "ctx"), None),
            P(("dp", "ctx")),
            P(("dp", "ctx"), None),
            P(None, ("dp", "ctx")),
            P(("dp", "ctx")),
            P(("dp", "ctx")),
            P(("dp", "ctx"), None),
            P(("dp", "ctx"), None),
            P(("dp", "ctx"), None),
            P(("dp", "ctx"), None),
            P(("dp", "ctx")),
            P(("dp", "ctx"), None),
            P(("dp", "ctx"), None),
            P(),
            P(),
            P(),
        ),
        check_vma=False,
    )
```
